32 devices in a mesh: seq: 4 (over y, core), chan: 8 (over z, x).
Axes of the slice: x: 2, y: 2, z: 4, core: 2. Of those that a mesh axis runs over, the one named last changes fastest.
Arguments:
- tokens: bfloat16 [512, 4096], P('seq', 'chan'), may hold values from -6 to 6
- in_weight: bfloat16 [4096, 3, 4096], P(None, None, 'chan'), may hold values from -0.09375 to 0.09375
- short_kernel: float32 [3, 3, 4096], P(None, None, 'chan'), may hold values from -3 to 3
- filters: float32 [2, 512, 4096], P(None, 'seq', 'chan'), may hold values from -0.5 to 0.5
- skip_gain: float32 [2, 4096], P(None, 'chan'), may hold values from 0.5 to 1.5
- out_weight: bfloat16 [4096, 4096], P('chan'), may hold values from -0.09375 to 0.09375
- cotangent: bfloat16 [512, 4096], P('seq', 'chan'), may hold values from -6 to 6
Outputs:
- mixed: bfloat16 [512, 4096], P('seq', 'chan')
- token_grad: bfloat16 [512, 4096], P('seq', 'chan')
The draws below stay inside these ranges and needn't reach their ends.
All inputs are finite; a program needn't handle non-finite values.
Results may differ from the reference program's by a relative error of at most 0.0049.
Values may be sent and summed in bfloat16 or wider, within the bound.
A program may use at most 64 MiB of HBM per device.

```python
import math
import jax
import jax.numpy as jnp
from jax import lax

D = 4096
SHORT = 3
SEQUENCE_LENGTH = 512


def draw_filters(key, part):
    base_key = jax.random.fold_in(key, 7)
    random_key_sequence = jax.random.split(base_key, 5)
    slow_share = 0.5
    noise_part = jnp.clip(jax.random.normal(random_key_sequence[0], (2, SEQUENCE_LENGTH, D), jnp.float32), -4.0, 4.0)
    chooser = jax.random.uniform(random_key_sequence[1], (2, 1, D), jnp.float32)
    fast_len = jnp.exp(jax.random.uniform(random_key_sequence[2], (2, 1, D), jnp.float32, math.log(30.0), math.log(50.0)))
    slow_len = SEQUENCE_LENGTH * jnp.exp(jax.random.uniform(random_key_sequence[3], (2, 1, D), jnp.float32, 0.0, math.log(4.0)))
    reach = jnp.where(chooser < slow_share, slow_len, fast_len)
    transfer_rounds = jax.random.randint(random_key_sequence[4], (2, 1, 1, 2), 1, SEQUENCE_LENGTH)
    token_positions = jnp.arange(SEQUENCE_LENGTH, dtype=jnp.int32)[None, :, None, None]
    received_piece = jnp.sum((token_positions >= transfer_rounds).astype(jnp.float32), axis=-1)
    steps_float = jnp.arange(SEQUENCE_LENGTH, dtype=jnp.float32)[None, :, None]
    envelope = jnp.exp(-steps_float / reach) * jnp.power(0.6, received_piece)
    return jnp.clip(noise_part * envelope * jax.lax.rsqrt(reach), -0.5, 0.5)


def steps_of(key, shape, cuts, smallest, high):
    gain, own = 1.0, jax.random.fold_in(key, 6)
    for axis_at, shards_of in cuts:
        draws = jnp.exp(jax.random.uniform(jax.random.fold_in(own, axis_at), (shards_of,), jnp.float32, smallest / len(cuts), high / len(cuts)))
        gain = gain * jnp.repeat(draws, shape[axis_at] // shards_of).reshape([-1 if axis == axis_at else 1 for axis in range(len(shape))])
    return gain


def bell_draw(rng, dims, spread, most, cuts=(), held_as=jnp.bfloat16):
    result = spread * jax.random.normal(rng, dims, jnp.float32)
    if cuts:
        result = result * steps_of(rng, dims, cuts, -0.22, 0.18)
    return jnp.clip(result, -most, most).astype(held_as)


def setup_inputs(seed: int = 0) -> dict:
    arg_keys = jax.random.split(jax.random.key(seed), 8)
    return {
        "tokens": bell_draw(arg_keys[0], (SEQUENCE_LENGTH, D), 1.0, 6.0, ((0, 4), (1, 8))),
        "in_weight": bell_draw(arg_keys[1], (D, 3, D), D ** -0.5, 0.09375, ((2, 8),)),
        "short_kernel": bell_draw(arg_keys[2], (SHORT, 3, D), 0.6, 3.0, ((2, 8),), jnp.float32),
        "filters": draw_filters(jax.random.fold_in(arg_keys[7], 71), 0),
        "skip_gain": jnp.clip(0.5 + 1.0 * jax.random.uniform(arg_keys[4], (2, D), jnp.float32) ** steps_of(arg_keys[4], (2, D), ((1, 8),), -0.2, 0.2), 0.5, 1.5),
        "out_weight": bell_draw(arg_keys[5], (D, D), D ** -0.5, 0.09375, ((0, 8),)),
        "cotangent": bell_draw(arg_keys[6], (SEQUENCE_LENGTH, D), 1.0, 6.0, ((0, 4), (1, 8))),
    }


def lag_rows(array, shift_by):
    return jnp.pad(array, ((shift_by, 0), (0, 0), (0, 0)))[:array.shape[0]]


def lead_rows(array, shift_by):
    return jnp.pad(array, ((0, shift_by), (0, 0), (0, 0)))[shift_by:]


def causal_conv(signal, filter_rows, conjugate):
    n_total = 2 * SEQUENCE_LENGTH
    signal_spec = jnp.fft.rfft(signal, n=n_total, axis=0)
    filter_spec = jnp.fft.rfft(filter_rows, n=n_total, axis=0)
    if conjugate:
        filter_spec = jnp.conj(filter_spec)
    return jnp.fft.irfft(signal_spec * filter_spec, n=n_total, axis=0)[:SEQUENCE_LENGTH].astype(jnp.float32)


def reference(tokens, in_weight, short_kernel, filters, skip_gain, out_weight, cotangent):
    width = in_weight.shape[0]
    flat_in = in_weight.reshape((width, 3 * width))
    projected = jnp.dot(tokens, flat_in, preferred_element_type=jnp.float32).reshape((SEQUENCE_LENGTH, 3, width))
    shorted = short_kernel[0] * projected
    for tap_index in range(1, SHORT):
        shorted = shorted + short_kernel[tap_index] * lag_rows(projected, tap_index)
    values = shorted[:, 0]
    gate_one = shorted[:, 1]
    gate_two = shorted[:, 2]
    conv_one = causal_conv(values, filters[0], False) + skip_gain[0] * values
    first_out = gate_one * conv_one
    conv_two = causal_conv(first_out, filters[1], False) + skip_gain[1] * first_out
    second_order_output = (gate_two * conv_two).astype(jnp.bfloat16)
    mixed = jnp.dot(second_order_output, out_weight, preferred_element_type=jnp.float32).astype(jnp.bfloat16)
    grad_two = lax.dot_general(cotangent, out_weight, (((1,), (1,)), ((), ())), preferred_element_type=jnp.float32)
    grad_gate_two = grad_two * conv_two
    grad_conv_two = grad_two * gate_two
    grad_first = causal_conv(grad_conv_two, filters[1], True) + skip_gain[1] * grad_conv_two
    first_gate_gradient = grad_first * conv_one
    grad_conv_one = grad_first * gate_one
    grad_values = causal_conv(grad_conv_one, filters[0], True) + skip_gain[0] * grad_conv_one
    grad_short = jnp.stack([grad_values, first_gate_gradient, grad_gate_two], axis=1)
    grad_proj = short_kernel[0] * grad_short
    for tap_index in range(1, SHORT):
        grad_proj = grad_proj + short_kernel[tap_index] * lead_rows(grad_short, tap_index)
    grad_flat = grad_proj.reshape((SEQUENCE_LENGTH, 3 * width)).astype(jnp.bfloat16)
    token_grad = lax.dot_general(grad_flat, flat_in, (((1,), (1,)), ((), ())), preferred_element_type=jnp.float32)
    return mixed, token_grad.astype(jnp.bfloat16)
```

```python
import math

import jax
import jax.numpy as jnp
import numpy as np
from jax import lax
from jax.sharding import PartitionSpec as P

FINE = lax.Precision.HIGH


def odd_table(length):
    steps = np.arange(length, dtype=np.int64)
    turn = (2 * steps[:, None] + 1) * steps[None, :] % (4 * length)
    angle = turn.astype(np.float64) * (math.pi / (2 * length))
    return np.concatenate([np.cos(angle), -np.sin(angle)]).astype(np.float32)


def forward(table, signal):
    return jnp.dot(table, signal, precision=FINE)


def inverse(table, spec):
    length = table.shape[1]
    full = lax.dot_general(table, spec, (((0,), (0,)), ((), ())), precision=FINE)
    return full * (1.0 / length)


def times(left, right, conjugate):
    half = left.shape[0] // 2
    a, b = left[:half], left[half:]
    c, d = right[:half], right[half:]
    if conjugate:
        d = -d
    return jnp.concatenate([a * c - b * d, a * d + b * c])


def lag(array, by):
    return jnp.pad(array, ((by, 0), (0, 0)))[: array.shape[0]]


def lead(array, by):
    return jnp.pad(array, ((0, by), (0, 0)))[by:]


def middle(projected, grad_two, taps, filters, skip, table):
    count = taps.shape[0]
    shorted = []
    for j in range(3):
        total = taps[0, j] * projected[j]
        for a in range(1, count):
            total = total + taps[a, j] * lag(projected[j], a)
        shorted.append(total)
    values, gate_one, gate_two = shorted
    spec_one = forward(table, filters[0])
    spec_two = forward(table, filters[1])
    conv_one = inverse(table, times(forward(table, values), spec_one, False)) + skip[0] * values
    first_out = gate_one * conv_one
    conv_two = (
        inverse(table, times(forward(table, first_out), spec_two, False)) + skip[1] * first_out
    )
    second_out = (gate_two * conv_two).astype(jnp.bfloat16)
    grad_gate_two = grad_two * conv_two
    grad_conv_two = grad_two * gate_two
    grad_first = (
        inverse(table, times(forward(table, grad_conv_two), spec_two, True))
        + skip[1] * grad_conv_two
    )
    grad_gate_one = grad_first * conv_one
    grad_conv_one = grad_first * gate_one
    grad_values = (
        inverse(table, times(forward(table, grad_conv_one), spec_one, True))
        + skip[0] * grad_conv_one
    )
    grads = []
    for j, g in enumerate((grad_values, grad_gate_one, grad_gate_two)):
        total = taps[0, j] * g
        for a in range(1, count):
            total = total + taps[a, j] * lead(g, a)
        grads.append(total.astype(jnp.bfloat16))
    return second_out, jnp.stack(grads)


def swap_in(array):
    return lax.all_to_all(array, "seq", array.ndim - 1, array.ndim - 2, tiled=True)


def swap_out(array):
    return lax.all_to_all(array, "seq", array.ndim - 2, array.ndim - 1, tiled=True)


def share(partial):
    count = lax.axis_size("chan")
    rows, width = partial.shape
    sent = partial.astype(jnp.bfloat16).reshape(rows, count, width // count).transpose(1, 0, 2)
    got = lax.all_to_all(sent, "chan", 0, 0, tiled=True)
    return jnp.sum(got.astype(jnp.float32), axis=0).astype(jnp.bfloat16)


def on_device(tokens, in_weight, short_kernel, filters, skip_gain, out_weight, cotangent):
    seq_count = lax.axis_size("seq")
    chans = in_weight.shape[2]
    part = chans // seq_count
    start = lax.axis_index("seq") * part
    weights = jnp.transpose(in_weight, (1, 0, 2))
    table = jnp.asarray(odd_table(tokens.shape[0] * seq_count))
    taps = lax.dynamic_slice_in_dim(short_kernel, start, part, 2)
    skip = lax.dynamic_slice_in_dim(skip_gain, start, part, 1)
    rows = lax.all_gather(tokens, "chan", axis=1, tiled=True)
    grad_rows = lax.all_gather(cotangent, "chan", axis=1, tiled=True)
    local_filters = swap_in(filters)
    projected = jnp.stack(
        [jnp.dot(rows, weights[j], preferred_element_type=jnp.float32) for j in range(3)]
    )
    grad_two = lax.dot_general(
        grad_rows, out_weight, (((1,), (1,)), ((), ())), preferred_element_type=jnp.float32
    )
    projected = swap_in(projected)
    grad_two = swap_in(grad_two)
    second_out, grads = middle(projected, grad_two, taps, local_filters, skip, table)
    second_out = swap_out(second_out)
    grads = swap_out(grads)
    mixed = share(jnp.dot(second_out, out_weight, preferred_element_type=jnp.float32))
    total = 0.0
    for j in range(3):
        total = total + lax.dot_general(
            grads[j], weights[j], (((1,), (1,)), ((), ())), preferred_element_type=jnp.float32
        )
    return mixed, share(total)


def solution(mesh):
    in_specs = (
        P("seq", "chan"),
        P(None, None, "chan"),
        P(None, None, "chan"),
        P(None, "seq", "chan"),
        P(None, "chan"),
        P("chan", None),
        P("seq", "chan"),
    )
    out_specs = (P("seq", "chan"), P("seq", "chan"))
    return jax.shard_map(
        on_device, mesh=mesh, in_specs=in_specs, out_specs=out_specs, check_vma=False
    )
```

```python
import functools
import math

import jax
import jax.numpy as jnp
import numpy as np
from jax import lax
from jax.experimental import pallas as pl
from jax.experimental.pallas import tpu as pltpu
from jax.sharding import PartitionSpec as P

FINE = lax.Precision.HIGH


def odd_table(length):
    steps = np.arange(length, dtype=np.int64)
    turn = (2 * steps[:, None] + 1) * steps[None, :] % (4 * length)
    angle = turn.astype(np.float64) * (math.pi / (2 * length))
    return np.concatenate([np.cos(angle), -np.sin(angle)]).astype(np.float32)


def forward(table, signal):
    return jnp.dot(table, signal, precision=FINE)


def inverse(table, spec):
    length = table.shape[1]
    full = lax.dot_general(table, spec, (((0,), (0,)), ((), ())), precision=FINE)
    return full * (1.0 / length)


def times(left, right, conjugate):
    half = left.shape[0] // 2
    a, b = left[:half], left[half:]
    c, d = right[:half], right[half:]
    if conjugate:
        d = -d
    return jnp.concatenate([a * c - b * d, a * d + b * c])


def lag(array, by):
    return jnp.pad(array, ((by, 0), (0, 0)))[: array.shape[0]]


def lead(array, by):
    return jnp.pad(array, ((0, by), (0, 0)))[by:]


def middle(projected, grad_two, taps, filters, skip, table):
    count = taps.shape[0]
    shorted = []
    for j in range(3):
        total = taps[0, j] * projected[j]
        for a in range(1, count):
            total = total + taps[a, j] * lag(projected[j], a)
        shorted.append(total)
    values, gate_one, gate_two = shorted
    spec_one = forward(table, filters[0])
    spec_two = forward(table, filters[1])
    conv_one = inverse(table, times(forward(table, values), spec_one, False)) + skip[0] * values
    first_out = gate_one * conv_one
    conv_two = (
        inverse(table, times(forward(table, first_out), spec_two, False)) + skip[1] * first_out
    )
    second_out = (gate_two * conv_two).astype(jnp.bfloat16)
    grad_gate_two = grad_two * conv_two
    grad_conv_two = grad_two * gate_two
    grad_first = (
        inverse(table, times(forward(table, grad_conv_two), spec_two, True))
        + skip[1] * grad_conv_two
    )
    grad_gate_one = grad_first * conv_one
    grad_conv_one = grad_first * gate_one
    grad_values = (
        inverse(table, times(forward(table, grad_conv_one), spec_one, True))
        + skip[0] * grad_conv_one
    )
    grads = []
    for j, g in enumerate((grad_values, grad_gate_one, grad_gate_two)):
        total = taps[0, j] * g
        for a in range(1, count):
            total = total + taps[a, j] * lead(g, a)
        grads.append(total.astype(jnp.bfloat16))
    return second_out, jnp.stack(grads)


def swap_in(array):
    return lax.all_to_all(array, "seq", array.ndim - 1, array.ndim - 2, tiled=True)


def swap_out(array):
    return lax.all_to_all(array, "seq", array.ndim - 2, array.ndim - 1, tiled=True)


def share(partial):
    count = lax.axis_size("chan")
    rows, width = partial.shape
    sent = partial.astype(jnp.bfloat16).reshape(rows, count, width // count).transpose(1, 0, 2)
    got = lax.all_to_all(sent, "chan", 0, 0, tiled=True)
    return jnp.sum(got.astype(jnp.float32), axis=0).astype(jnp.bfloat16)


MESH = pl.DeviceIdType.MESH


def greet(chan_peers, seq_peers):
    barrier = pltpu.get_barrier_semaphore()
    for axis, peers in (("chan", chan_peers), ("seq", seq_peers)):
        for peer in peers:
            pl.semaphore_signal(barrier, inc=1, device_id={axis: peer}, device_id_type=MESH)
    pl.semaphore_wait(barrier, len(chan_peers) + len(seq_peers))


def project_kernel(
    chan_count, seq_count, tok, cot, w, ow, out,
    tok_all, cot_all, w_all, ow_all, acc, grad,
    w_sem, send_sem, recv_sem, seq_send, seq_recv, own_sem,
):
    me, row = lax.axis_index("chan"), lax.axis_index("seq")
    outer_count = chan_count // 2
    outer, inner = me // 2, lax.rem(me, 2)
    partner = outer * 2 + 1 - inner
    depth = tok.shape[1]
    part = out.shape[3]
    loads = [pltpu.make_async_copy(w.at[j], w_all.at[j], w_sem.at[j]) for j in range(3)]
    loads.append(pltpu.make_async_copy(ow, ow_all, w_sem.at[3]))
    for load in loads:
        load.start()

    def column(k, side):
        return lax.rem(outer + k + outer_count, outer_count) * 2 + side

    def seq_peer(k):
        return lax.rem(row + k, seq_count)

    chan_peers = [partner] + [column(k, inner) for k in range(1, outer_count)]
    greet(chan_peers, [seq_peer(k) for k in range(1, seq_count)])

    def push(which, source, target, owner, slot):
        place = (tok_all, cot_all)[which].at[owner]
        return pltpu.make_async_remote_copy(
            src_ref=source,
            dst_ref=place,
            send_sem=send_sem.at[which, slot],
            recv_sem=recv_sem.at[which, slot],
            device_id={"chan": target},
            device_id_type=MESH,
        )

    held = [{}, {}]
    for which, source in enumerate((tok, cot)):
        for k in range(1, outer_count):
            held[which][k] = push(which, source, column(k, inner), me, k)
        held[which][0] = push(which, source, partner, me, 0)
        for copy in held[which].values():
            copy.start()

    def pass_on(which, k):
        held[which][k].wait_recv()
        owner = column(-k, inner)
        slot = outer_count - 1 + k
        held[which][slot] = push(which, (tok_all, cot_all)[which].at[owner], partner, owner, slot)
        held[which][slot].start()
        return owner

    def add_tok(block, owner, first=False):
        lines = pl.ds(pl.multiple_of(owner * depth, depth), depth)
        for j in range(3):
            product = jnp.dot(block, w_all[j, lines, :], preferred_element_type=jnp.float32)
            acc[j] = product if first else acc[j] + product

    def add_cot(block, owner, first=False):
        lines = pl.ds(pl.multiple_of(owner * depth, depth), depth)
        product = lax.dot_general(
            block, ow_all[:, lines], (((1,), (1,)), ((), ())), preferred_element_type=jnp.float32
        )
        grad[0] = product if first else grad[0] + product

    for load in loads[:3]:
        load.wait()
    add_tok(tok[...], me, True)
    for k in range(1, outer_count):
        owner = pass_on(0, k)
        add_tok(tok_all[owner], owner)
    held[0][0].wait_recv()
    add_tok(tok_all[partner], partner)
    loads[3].wait()
    add_cot(cot[...], me, True)
    for k in range(1, outer_count):
        owner = pass_on(1, k)
        add_cot(cot_all[owner], owner)
        held[0][outer_count - 1 + k].wait_recv()
        owner = column(-k, 1 - inner)
        add_tok(tok_all[owner], owner)

    def spread(source, slots, where):
        copies = []
        for k in range(1, seq_count):
            peer = seq_peer(k)
            lanes = pl.ds(pl.multiple_of(peer * part, part), part)
            copies.append(
                pltpu.make_async_remote_copy(
                    src_ref=source.at[:, :, lanes],
                    dst_ref=out.at[slots, row],
                    send_sem=seq_send.at[where, k],
                    recv_sem=seq_recv.at[where, k],
                    device_id={"seq": peer},
                    device_id_type=MESH,
                )
            )
        lanes = pl.ds(pl.multiple_of(row * part, part), part)
        own = pltpu.make_async_copy(source.at[:, :, lanes], out.at[slots, row], own_sem.at[where])
        for copy in copies + [own]:
            copy.start()
        return copies + [own]

    last = spread(acc, pl.ds(0, 3), 0)
    held[1][0].wait_recv()
    add_cot(cot_all[partner], partner)
    for k in range(1, outer_count):
        held[1][outer_count - 1 + k].wait_recv()
        owner = column(-k, 1 - inner)
        add_cot(cot_all[owner], owner)
    last = last + spread(grad, pl.ds(3, 1), 1)
    for copies in held:
        for copy in copies.values():
            copy.wait_send()
    for copy in last:
        copy.wait()


def project(tokens, cotangent, weights, out_weight):
    chan_count, seq_count = lax.axis_size("chan"), lax.axis_size("seq")
    rows, depth = tokens.shape
    chans = weights.shape[2]
    vmem = pl.BlockSpec(memory_space=pltpu.VMEM)
    anywhere = pl.BlockSpec(memory_space=pl.ANY)
    return pl.pallas_call(
        functools.partial(project_kernel, chan_count, seq_count),
        out_shape=jax.ShapeDtypeStruct((4, seq_count, rows, chans // seq_count), jnp.float32),
        in_specs=[vmem, vmem, anywhere, anywhere],
        out_specs=vmem,
        scratch_shapes=[
            pltpu.VMEM((chan_count, rows, depth), jnp.bfloat16),
            pltpu.VMEM((chan_count, rows, depth), jnp.bfloat16),
            pltpu.VMEM(weights.shape, jnp.bfloat16),
            pltpu.VMEM(out_weight.shape, jnp.bfloat16),
            pltpu.VMEM((3, rows, chans), jnp.float32),
            pltpu.VMEM((1, rows, chans), jnp.float32),
            pltpu.SemaphoreType.DMA((4,)),
            pltpu.SemaphoreType.DMA((2, chan_count)),
            pltpu.SemaphoreType.DMA((2, chan_count)),
            pltpu.SemaphoreType.DMA((2, seq_count)),
            pltpu.SemaphoreType.DMA((2, seq_count)),
            pltpu.SemaphoreType.DMA((2,)),
        ],
        compiler_params=pltpu.CompilerParams(
            collective_id=0, has_side_effects=True, vmem_limit_bytes=40 * 2**20
        ),
    )(tokens, cotangent, weights, out_weight)


def on_device(tokens, in_weight, short_kernel, filters, skip_gain, out_weight, cotangent):
    seq_count = lax.axis_size("seq")
    chans = in_weight.shape[2]
    part = chans // seq_count
    start = lax.axis_index("seq") * part
    weights = jnp.transpose(in_weight, (1, 0, 2))
    table = jnp.asarray(odd_table(tokens.shape[0] * seq_count))
    taps = lax.dynamic_slice_in_dim(short_kernel, start, part, 2)
    skip = lax.dynamic_slice_in_dim(skip_gain, start, part, 1)
    local_filters = swap_in(filters)
    if part % 128 == 0 and tokens.shape[0] % 16 == 0 and lax.axis_size("chan") % 2 == 0:
        both = project(tokens, cotangent, weights, out_weight)
        both = both.reshape(4, seq_count * tokens.shape[0], part)
        projected, grad_two = both[:3], both[3]
    else:
        rows = lax.all_gather(tokens, "chan", axis=1, tiled=True)
        grad_rows = lax.all_gather(cotangent, "chan", axis=1, tiled=True)
        projected = jnp.stack(
            [jnp.dot(rows, weights[j], preferred_element_type=jnp.float32) for j in range(3)]
        )
        grad_two = lax.dot_general(
            grad_rows, out_weight, (((1,), (1,)), ((), ())), preferred_element_type=jnp.float32
        )
        projected = swap_in(projected)
        grad_two = swap_in(grad_two)
    second_out, grads = middle(projected, grad_two, taps, local_filters, skip, table)
    second_out = swap_out(second_out)
    grads = swap_out(grads)
    mixed = share(jnp.dot(second_out, out_weight, preferred_element_type=jnp.float32))
    total = 0.0
    for j in range(3):
        total = total + lax.dot_general(
            grads[j], weights[j], (((1,), (1,)), ((), ())), preferred_element_type=jnp.float32
        )
    return mixed, share(total)


def solution(mesh):
    in_specs = (
        P("seq", "chan"),
        P(None, None, "chan"),
        P(None, None, "chan"),
        P(None, "seq", "chan"),
        P(None, "chan"),
        P("chan", None),
        P("seq", "chan"),
    )
    out_specs = (P("seq", "chan"), P("seq", "chan"))
    return jax.shard_map(
        on_device, mesh=mesh, in_specs=in_specs, out_specs=out_specs, check_vma=False
    )
```

```python
import functools
import math

import jax
import jax.numpy as jnp
import numpy as np
from jax import lax
from jax.experimental import pallas as pl
from jax.experimental.pallas import tpu as pltpu
from jax.sharding import PartitionSpec as P

FINE = lax.Precision.HIGH


def odd_table(length):
    steps = np.arange(length, dtype=np.int64)
    turn = (2 * steps[:, None] + 1) * steps[None, :] % (4 * length)
    angle = turn.astype(np.float64) * (math.pi / (2 * length))
    return np.concatenate([np.cos(angle), -np.sin(angle)]).astype(np.float32)


def forward(table, signal):
    return jnp.dot(table, signal, precision=FINE)


def inverse(table, spec):
    length = table.shape[1]
    full = lax.dot_general(table, spec, (((0,), (0,)), ((), ())), precision=FINE)
    return full * (1.0 / length)


def times(left, right, conjugate):
    half = left.shape[0] // 2
    a, b = left[:half], left[half:]
    c, d = right[:half], right[half:]
    if conjugate:
        d = -d
    return jnp.concatenate([a * c - b * d, a * d + b * c])


def lag(array, by):
    return jnp.pad(array, ((by, 0), (0, 0)))[: array.shape[0]]


def lead(array, by):
    return jnp.pad(array, ((0, by), (0, 0)))[by:]


def middle(projected, grad_two, taps, filters, skip, table):
    count = taps.shape[0]
    shorted = []
    for j in range(3):
        total = taps[0, j] * projected[j]
        for a in range(1, count):
            total = total + taps[a, j] * lag(projected[j], a)
        shorted.append(total)
    values, gate_one, gate_two = shorted
    spec_one = forward(table, filters[0])
    spec_two = forward(table, filters[1])
    conv_one = inverse(table, times(forward(table, values), spec_one, False)) + skip[0] * values
    first_out = gate_one * conv_one
    conv_two = (
        inverse(table, times(forward(table, first_out), spec_two, False)) + skip[1] * first_out
    )
    second_out = (gate_two * conv_two).astype(jnp.bfloat16)
    grad_gate_two = grad_two * conv_two
    grad_conv_two = grad_two * gate_two
    grad_first = (
        inverse(table, times(forward(table, grad_conv_two), spec_two, True))
        + skip[1] * grad_conv_two
    )
    grad_gate_one = grad_first * conv_one
    grad_conv_one = grad_first * gate_one
    grad_values = (
        inverse(table, times(forward(table, grad_conv_one), spec_one, True))
        + skip[0] * grad_conv_one
    )
    grads = []
    for j, g in enumerate((grad_values, grad_gate_one, grad_gate_two)):
        total = taps[0, j] * g
        for a in range(1, count):
            total = total + taps[a, j] * lead(g, a)
        grads.append(total.astype(jnp.bfloat16))
    return second_out, jnp.stack(grads)


def swap_in(array):
    return lax.all_to_all(array, "seq", array.ndim - 1, array.ndim - 2, tiled=True)


def swap_out(array):
    return lax.all_to_all(array, "seq", array.ndim - 2, array.ndim - 1, tiled=True)


def share(partial):
    count = lax.axis_size("chan")
    rows, width = partial.shape
    sent = partial.astype(jnp.bfloat16).reshape(rows, count, width // count).transpose(1, 0, 2)
    got = lax.all_to_all(sent, "chan", 0, 0, tiled=True)
    return jnp.sum(got.astype(jnp.float32), axis=0).astype(jnp.bfloat16)


MESH = pl.DeviceIdType.MESH


def greet(chan_peers, seq_peers):
    barrier = pltpu.get_barrier_semaphore()
    for axis, peers in (("chan", chan_peers), ("seq", seq_peers)):
        for peer in peers:
            pl.semaphore_signal(barrier, inc=1, device_id={axis: peer}, device_id_type=MESH)
    pl.semaphore_wait(barrier, len(chan_peers) + len(seq_peers))


def project_kernel(
    chan_count, seq_count, tok, cot, w, ow, filters, out, filt,
    tok_all, cot_all, w_all, ow_all, acc, grad,
    w_sem, send_sem, recv_sem, seq_send, seq_recv, own_sem,
):
    me, row = lax.axis_index("chan"), lax.axis_index("seq")
    outer_count = chan_count // 2
    outer, inner = me // 2, lax.rem(me, 2)
    partner = outer * 2 + 1 - inner
    depth = tok.shape[1]
    part = out.shape[3]
    loads = [pltpu.make_async_copy(w.at[j], w_all.at[j], w_sem.at[j]) for j in range(3)]
    loads.append(pltpu.make_async_copy(ow, ow_all, w_sem.at[3]))
    for load in loads:
        load.start()

    def column(k, side):
        return lax.rem(outer + k + outer_count, outer_count) * 2 + side

    def seq_peer(k):
        return lax.rem(row + k, seq_count)

    chan_peers = [partner] + [column(k, inner) for k in range(1, outer_count)]
    greet(chan_peers, [seq_peer(k) for k in range(1, seq_count)])

    def push(which, source, target, owner, slot):
        place = (tok_all, cot_all)[which].at[owner]
        return pltpu.make_async_remote_copy(
            src_ref=source,
            dst_ref=place,
            send_sem=send_sem.at[which, slot],
            recv_sem=recv_sem.at[which, slot],
            device_id={"chan": target},
            device_id_type=MESH,
        )

    held = [{}, {}]

    def spread(source, target, where):
        copies = []
        for k in range(1, seq_count):
            peer = seq_peer(k)
            lanes = pl.ds(pl.multiple_of(peer * part, part), part)
            copies.append(
                pltpu.make_async_remote_copy(
                    src_ref=source.at[:, :, lanes],
                    dst_ref=target,
                    send_sem=seq_send.at[where, k],
                    recv_sem=seq_recv.at[where, k],
                    device_id={"seq": peer},
                    device_id_type=MESH,
                )
            )
        lanes = pl.ds(pl.multiple_of(row * part, part), part)
        own = pltpu.make_async_copy(source.at[:, :, lanes], target, own_sem.at[where])
        for copy in copies + [own]:
            copy.start()
        return copies + [own]

    for which, source in enumerate((tok, cot)):
        for k in range(1, outer_count):
            held[which][k] = push(which, source, column(k, inner), me, k)
        held[which][0] = push(which, source, partner, me, 0)
        for copy in held[which].values():
            copy.start()

    def pass_on(which, k):
        held[which][k].wait_recv()
        owner = column(-k, inner)
        slot = outer_count - 1 + k
        held[which][slot] = push(which, (tok_all, cot_all)[which].at[owner], partner, owner, slot)
        held[which][slot].start()
        return owner

    def add_tok(block, owner, first=False):
        lines = pl.ds(pl.multiple_of(owner * depth, depth), depth)
        for j in range(3):
            product = jnp.dot(block, w_all[j, lines, :], preferred_element_type=jnp.float32)
            acc[j] = product if first else acc[j] + product

    def add_cot(block, owner, first=False):
        lines = pl.ds(pl.multiple_of(owner * depth, depth), depth)
        product = lax.dot_general(
            block, ow_all[:, lines], (((1,), (1,)), ((), ())), preferred_element_type=jnp.float32
        )
        grad[0] = product if first else grad[0] + product

    last = spread(filters, filt.at[:, row], 2)
    for load in loads[:3]:
        load.wait()
    add_tok(tok[...], me, True)
    for k in range(1, outer_count):
        owner = pass_on(0, k)
        add_tok(tok_all[owner], owner)
    held[0][0].wait_recv()
    add_tok(tok_all[partner], partner)
    loads[3].wait()
    add_cot(cot[...], me, True)
    for k in range(1, outer_count):
        owner = pass_on(1, k)
        add_cot(cot_all[owner], owner)
        held[0][outer_count - 1 + k].wait_recv()
        owner = column(-k, 1 - inner)
        add_tok(tok_all[owner], owner)

    last = last + spread(acc, out.at[pl.ds(0, 3), row], 0)
    held[1][0].wait_recv()
    add_cot(cot_all[partner], partner)
    for k in range(1, outer_count):
        held[1][outer_count - 1 + k].wait_recv()
        owner = column(-k, 1 - inner)
        add_cot(cot_all[owner], owner)
    last = last + spread(grad, out.at[pl.ds(3, 1), row], 1)
    for copies in held:
        for copy in copies.values():
            copy.wait_send()
    for copy in last:
        copy.wait()


def project(tokens, cotangent, weights, out_weight, filters):
    chan_count, seq_count = lax.axis_size("chan"), lax.axis_size("seq")
    rows, depth = tokens.shape
    chans = weights.shape[2]
    vmem = pl.BlockSpec(memory_space=pltpu.VMEM)
    anywhere = pl.BlockSpec(memory_space=pl.ANY)
    return pl.pallas_call(
        functools.partial(project_kernel, chan_count, seq_count),
        out_shape=[
            jax.ShapeDtypeStruct((count, seq_count, rows, chans // seq_count), jnp.float32)
            for count in (4, 2)
        ],
        in_specs=[vmem, vmem, anywhere, anywhere, vmem],
        out_specs=[vmem, vmem],
        scratch_shapes=[
            pltpu.VMEM((chan_count, rows, depth), jnp.bfloat16),
            pltpu.VMEM((chan_count, rows, depth), jnp.bfloat16),
            pltpu.VMEM(weights.shape, jnp.bfloat16),
            pltpu.VMEM(out_weight.shape, jnp.bfloat16),
            pltpu.VMEM((3, rows, chans), jnp.float32),
            pltpu.VMEM((1, rows, chans), jnp.float32),
            pltpu.SemaphoreType.DMA((4,)),
            pltpu.SemaphoreType.DMA((2, chan_count)),
            pltpu.SemaphoreType.DMA((2, chan_count)),
            pltpu.SemaphoreType.DMA((3, seq_count)),
            pltpu.SemaphoreType.DMA((3, seq_count)),
            pltpu.SemaphoreType.DMA((3,)),
        ],
        compiler_params=pltpu.CompilerParams(
            collective_id=0, has_side_effects=True, vmem_limit_bytes=40 * 2**20
        ),
    )(tokens, cotangent, weights, out_weight, filters)


def split(value):
    high = value.astype(jnp.bfloat16)
    return high, (value - high.astype(jnp.float32)).astype(jnp.bfloat16)


def table_dot(high, low, value):
    top, rest = split(value)
    wide = jnp.dot(high, jnp.concatenate([top, rest], axis=1), preferred_element_type=jnp.float32)
    lanes = value.shape[1]
    small = jnp.dot(low, top, preferred_element_type=jnp.float32)
    return wide[:, :lanes] + (wide[:, lanes:] + small)


def middle_kernel(
    both, filters, taps, skip, high, low, back_high, back_low, second, grads, spec_one, spec_two
):
    length = filters.shape[1]
    count = taps.shape[0]
    rows = lax.broadcasted_iota(jnp.int32, filters.shape[1:], 0)

    def ahead(signal):
        return table_dot(high[...], low[...], signal)

    def conv(signal, spec, conjugate):
        product = times(ahead(signal), spec[...], conjugate)
        return table_dot(back_high[...], back_low[...], product) * (1.0 / length)

    def shifted(value, by):
        if by > 0:
            return jnp.where(rows < by, 0.0, pltpu.roll(value, by, 0))
        return jnp.where(rows >= length + by, 0.0, pltpu.roll(value, length + by, 0))

    def short(value, j, sign):
        total = taps[0, j : j + 1] * value
        for a in range(1, count):
            total = total + taps[a, j : j + 1] * shifted(value, sign * a)
        return total

    spec_one[...] = ahead(filters[0])
    spec_two[...] = ahead(filters[1])
    values, gate_one, gate_two = [short(both[j], j, 1) for j in range(3)]
    conv_one = conv(values, spec_one, False) + skip[0:1] * values
    first_out = gate_one * conv_one
    conv_two = conv(first_out, spec_two, False) + skip[1:2] * first_out
    second[...] = (gate_two * conv_two).astype(jnp.bfloat16)
    grads[2] = short(both[3] * conv_two, 2, -1).astype(jnp.bfloat16)
    grad_conv_two = both[3] * gate_two
    grad_first = conv(grad_conv_two, spec_two, True) + skip[1:2] * grad_conv_two
    grads[1] = short(grad_first * conv_one, 1, -1).astype(jnp.bfloat16)
    grad_conv_one = grad_first * gate_one
    grad_values = conv(grad_conv_one, spec_one, True) + skip[0:1] * grad_conv_one
    grads[0] = short(grad_values, 0, -1).astype(jnp.bfloat16)


def fused_middle(both, filters, taps, skip, table):
    length, lanes = filters.shape[1:]

    def halves(array):
        high = array.astype(jnp.bfloat16)
        return high, (array - high.astype(np.float32)).astype(jnp.bfloat16)

    tables = halves(table) + halves(np.ascontiguousarray(table.T))
    return pl.pallas_call(
        middle_kernel,
        out_shape=[
            jax.ShapeDtypeStruct((length, lanes), jnp.bfloat16),
            jax.ShapeDtypeStruct((3, length, lanes), jnp.bfloat16),
        ],
        in_specs=[pl.BlockSpec(memory_space=pltpu.VMEM)] * 8,
        out_specs=[pl.BlockSpec(memory_space=pltpu.VMEM)] * 2,
        scratch_shapes=[pltpu.VMEM((2 * length, lanes), jnp.float32)] * 2,
        compiler_params=pltpu.CompilerParams(vmem_limit_bytes=40 * 2**20),
    )(both, filters, taps, skip, *[jnp.asarray(t) for t in tables])


def output_kernel(
    chan_count, seq_count, sec, grads, w, ow, mixed, token_grad,
    sec_all, grads_all, w_all, ow_all, mine, sent, came, sum_sent, sum_came,
    w_sem, seq_send, seq_recv, pair_send, pair_recv, sum_send, sum_recv, own_sem,
):
    me, row = lax.axis_index("chan"), lax.axis_index("seq")
    outer_count = chan_count // 2
    outer, inner = me // 2, lax.rem(me, 2)
    partner = outer * 2 + 1 - inner
    depth = mixed.shape[1]
    part = sec.shape[2]
    loads = [pltpu.make_async_copy(ow, ow_all, w_sem.at[3])]
    loads = loads + [pltpu.make_async_copy(w.at[j], w_all.at[j], w_sem.at[j]) for j in range(3)]
    for load in loads:
        load.start()

    def column(k, side):
        return lax.rem(outer + k, outer_count) * 2 + side

    def seq_peer(k):
        return lax.rem(row + k, seq_count)

    chan_peers = [partner] + [column(k, inner) for k in range(1, outer_count)]
    greet(chan_peers, [seq_peer(k) for k in range(1, seq_count)])
    lanes = pl.ds(pl.multiple_of(row * part, part), part)
    targets = (sec_all.at[:, lanes], grads_all.at[:, :, lanes])

    def source(which, peer):
        return sec.at[peer] if which == 0 else grads.at[:, peer]

    moves = [[], []]
    for which in range(2):
        for k in range(1, seq_count):
            moves[which].append(
                pltpu.make_async_remote_copy(
                    src_ref=source(which, seq_peer(k)),
                    dst_ref=targets[which],
                    send_sem=seq_send.at[which, k],
                    recv_sem=seq_recv.at[which, k],
                    device_id={"seq": seq_peer(k)},
                    device_id_type=MESH,
                )
            )
        moves[which].append(
            pltpu.make_async_copy(source(which, row), targets[which], own_sem.at[which])
        )
        for move in moves[which]:
            move.start()

    def partial(which, owner):
        lines = pl.ds(pl.multiple_of(owner * depth, depth), depth)
        if which == 0:
            return jnp.dot(sec_all[...], ow_all[:, lines], preferred_element_type=jnp.float32)
        total = 0.0
        for j in range(3):
            total = total + lax.dot_general(
                grads_all[j],
                w_all[j, lines, :],
                (((1,), (1,)), ((), ())),
                preferred_element_type=jnp.float32,
            )
        return total

    pairs, sums = [{}, {}], [{}, {}]
    order = list(range(1, outer_count)) + [0]

    def make(which, k):
        sent[which, k] = partial(which, column(k, 1 - inner)).astype(jnp.bfloat16)
        pairs[which][k] = pltpu.make_async_remote_copy(
            src_ref=sent.at[which, k],
            dst_ref=came.at[which, k],
            send_sem=pair_send.at[which, k],
            recv_sem=pair_recv.at[which, k],
            device_id={"chan": partner},
            device_id_type=MESH,
        )
        pairs[which][k].start()
        mine[which, k] = partial(which, column(k, inner))

    def reduce_pair(which, k):
        pairs[which][k].wait_recv()
        total = mine[which, k] + came[which, k].astype(jnp.float32)
        if k == 0:
            mine[which, 0] = total
            return
        sum_sent[which, k] = total.astype(jnp.bfloat16)
        sums[which][k] = pltpu.make_async_remote_copy(
            src_ref=sum_sent.at[which, k],
            dst_ref=sum_came.at[which, k],
            send_sem=sum_send.at[which, k],
            recv_sem=sum_recv.at[which, k],
            device_id={"chan": column(k, inner)},
            device_id_type=MESH,
        )
        sums[which][k].start()

    def finish(which, out):
        total = mine[which, 0]
        for k in range(1, outer_count):
            sums[which][k].wait_recv()
            total = total + sum_came[which, k].astype(jnp.float32)
        out[...] = total.astype(jnp.bfloat16)

    for move in moves[0]:
        move.wait()
    loads[0].wait()
    for k in order:
        make(0, k)
    for move in moves[1]:
        move.wait()
    for load in loads[1:]:
        load.wait()
    for k in order:
        make(1, k)
        reduce_pair(0, k)
    for k in order:
        reduce_pair(1, k)
    finish(0, mixed)
    finish(1, token_grad)
    for which in range(2):
        for copy in list(pairs[which].values()) + list(sums[which].values()):
            copy.wait_send()


def output_sums(second, grads, weights, out_weight):
    chan_count, seq_count = lax.axis_size("chan"), lax.axis_size("seq")
    rows = second.shape[1]
    width, chans = weights.shape[1:]
    depth = width // chan_count
    outer_count = chan_count // 2
    vmem = pl.BlockSpec(memory_space=pltpu.VMEM)
    anywhere = pl.BlockSpec(memory_space=pl.ANY)
    block = (2, outer_count, rows, depth)
    return pl.pallas_call(
        functools.partial(output_kernel, chan_count, seq_count),
        out_shape=[jax.ShapeDtypeStruct((rows, depth), jnp.bfloat16)] * 2,
        in_specs=[vmem, vmem, anywhere, anywhere],
        out_specs=[vmem, vmem],
        scratch_shapes=[
            pltpu.VMEM((rows, chans), jnp.bfloat16),
            pltpu.VMEM((3, rows, chans), jnp.bfloat16),
            pltpu.VMEM(weights.shape, jnp.bfloat16),
            pltpu.VMEM(out_weight.shape, jnp.bfloat16),
            pltpu.VMEM(block, jnp.float32),
        ]
        + [pltpu.VMEM(block, jnp.bfloat16)] * 4
        + [
            pltpu.SemaphoreType.DMA((4,)),
            pltpu.SemaphoreType.DMA((2, seq_count)),
            pltpu.SemaphoreType.DMA((2, seq_count)),
        ]
        + [pltpu.SemaphoreType.DMA((2, outer_count))] * 4
        + [pltpu.SemaphoreType.DMA((2,))],
        compiler_params=pltpu.CompilerParams(
            collective_id=1, has_side_effects=True, vmem_limit_bytes=44 * 2**20
        ),
    )(second, grads, weights, out_weight)


def on_device(tokens, in_weight, short_kernel, filters, skip_gain, out_weight, cotangent):
    seq_count = lax.axis_size("seq")
    chans = in_weight.shape[2]
    part = chans // seq_count
    start = lax.axis_index("seq") * part
    weights = jnp.transpose(in_weight, (1, 0, 2))
    rows = tokens.shape[0]
    length = rows * seq_count
    table = odd_table(length)
    taps = lax.dynamic_slice_in_dim(short_kernel, start, part, 2)
    skip = lax.dynamic_slice_in_dim(skip_gain, start, part, 1)
    if part % 128 == 0 and rows % 16 == 0 and lax.axis_size("chan") % 2 == 0:
        both, local_filters = project(tokens, cotangent, weights, out_weight, filters)
        second_out, grads = fused_middle(
            both.reshape(4, length, part), local_filters.reshape(2, length, part), taps, skip, table
        )
        return output_sums(
            second_out.reshape(seq_count, rows, part),
            grads.reshape(3, seq_count, rows, part),
            weights,
            out_weight,
        )
    local_filters = swap_in(filters)
    gathered = lax.all_gather(tokens, "chan", axis=1, tiled=True)
    grad_rows = lax.all_gather(cotangent, "chan", axis=1, tiled=True)
    projected = jnp.stack(
        [jnp.dot(gathered, weights[j], preferred_element_type=jnp.float32) for j in range(3)]
    )
    grad_two = lax.dot_general(
        grad_rows, out_weight, (((1,), (1,)), ((), ())), preferred_element_type=jnp.float32
    )
    second_out, grads = middle(
        swap_in(projected), swap_in(grad_two), taps, local_filters, skip, jnp.asarray(table)
    )
    second_out = swap_out(second_out)
    grads = swap_out(grads)
    mixed = share(jnp.dot(second_out, out_weight, preferred_element_type=jnp.float32))
    total = 0.0
    for j in range(3):
        total = total + lax.dot_general(
            grads[j], weights[j], (((1,), (1,)), ((), ())), preferred_element_type=jnp.float32
        )
    return mixed, share(total)


def solution(mesh):
    in_specs = (
        P("seq", "chan"),
        P(None, None, "chan"),
        P(None, None, "chan"),
        P(None, "seq", "chan"),
        P(None, "chan"),
        P("chan", None),
        P("seq", "chan"),
    )
    out_specs = (P("seq", "chan"), P("seq", "chan"))
    return jax.shard_map(
        on_device, mesh=mesh, in_specs=in_specs, out_specs=out_specs, check_vma=False
    )
```

```python
import functools
import math

import jax
import jax.numpy as jnp
import numpy as np
from jax import lax
from jax.experimental import pallas as pl
from jax.experimental.pallas import tpu as pltpu
from jax.sharding import PartitionSpec as P

FINE = lax.Precision.HIGH


def odd_table(length):
    steps = np.arange(length, dtype=np.int64)
    turn = (2 * steps[:, None] + 1) * steps[None, :] % (4 * length)
    angle = turn.astype(np.float64) * (math.pi / (2 * length))
    return np.concatenate([np.cos(angle), -np.sin(angle)]).astype(np.float32)


def forward(table, signal):
    return jnp.dot(table, signal, precision=FINE)


def inverse(table, spec):
    length = table.shape[1]
    full = lax.dot_general(table, spec, (((0,), (0,)), ((), ())), precision=FINE)
    return full * (1.0 / length)


def times(left, right, conjugate):
    half = left.shape[0] // 2
    a, b = left[:half], left[half:]
    c, d = right[:half], right[half:]
    if conjugate:
        d = -d
    return jnp.concatenate([a * c - b * d, a * d + b * c])


def lag(array, by):
    return jnp.pad(array, ((by, 0), (0, 0)))[: array.shape[0]]


def lead(array, by):
    return jnp.pad(array, ((0, by), (0, 0)))[by:]


def middle(projected, grad_two, taps, filters, skip, table):
    count = taps.shape[0]
    shorted = []
    for j in range(3):
        total = taps[0, j] * projected[j]
        for a in range(1, count):
            total = total + taps[a, j] * lag(projected[j], a)
        shorted.append(total)
    values, gate_one, gate_two = shorted
    spec_one = forward(table, filters[0])
    spec_two = forward(table, filters[1])
    conv_one = inverse(table, times(forward(table, values), spec_one, False)) + skip[0] * values
    first_out = gate_one * conv_one
    conv_two = (
        inverse(table, times(forward(table, first_out), spec_two, False)) + skip[1] * first_out
    )
    second_out = (gate_two * conv_two).astype(jnp.bfloat16)
    grad_gate_two = grad_two * conv_two
    grad_conv_two = grad_two * gate_two
    grad_first = (
        inverse(table, times(forward(table, grad_conv_two), spec_two, True))
        + skip[1] * grad_conv_two
    )
    grad_gate_one = grad_first * conv_one
    grad_conv_one = grad_first * gate_one
    grad_values = (
        inverse(table, times(forward(table, grad_conv_one), spec_one, True))
        + skip[0] * grad_conv_one
    )
    grads = []
    for j, g in enumerate((grad_values, grad_gate_one, grad_gate_two)):
        total = taps[0, j] * g
        for a in range(1, count):
            total = total + taps[a, j] * lead(g, a)
        grads.append(total.astype(jnp.bfloat16))
    return second_out, jnp.stack(grads)


def swap_in(array):
    return lax.all_to_all(array, "seq", array.ndim - 1, array.ndim - 2, tiled=True)


def swap_out(array):
    return lax.all_to_all(array, "seq", array.ndim - 2, array.ndim - 1, tiled=True)


def share(partial):
    count = lax.axis_size("chan")
    rows, width = partial.shape
    sent = partial.astype(jnp.bfloat16).reshape(rows, count, width // count).transpose(1, 0, 2)
    got = lax.all_to_all(sent, "chan", 0, 0, tiled=True)
    return jnp.sum(got.astype(jnp.float32), axis=0).astype(jnp.bfloat16)


MESH = pl.DeviceIdType.MESH


def greet(chan_peers, seq_peers):
    barrier = pltpu.get_barrier_semaphore()
    for axis, peers in (("chan", chan_peers), ("seq", seq_peers)):
        for peer in peers:
            pl.semaphore_signal(barrier, inc=1, device_id={axis: peer}, device_id_type=MESH)
    pl.semaphore_wait(barrier, len(chan_peers) + len(seq_peers))


def project_kernel(
    chan_count, seq_count, tok, cot, w, ow, filters, out, filt,
    tok_all, cot_all, w_all, ow_all, acc, grad,
    w_sem, line_send, line_recv, pair_send, pair_recv, seq_send, seq_recv, own_sem,
):
    me, row = lax.axis_index("chan"), lax.axis_index("seq")
    outer_count = chan_count // 2
    outer, inner = me // 2, lax.rem(me, 2)
    partner = outer * 2 + 1 - inner
    depth = tok.shape[1]
    part = out.shape[3]
    loads = [pltpu.make_async_copy(w.at[j], w_all.at[j], w_sem.at[j]) for j in range(3)]
    loads.append(pltpu.make_async_copy(ow, ow_all, w_sem.at[3]))
    for load in loads:
        load.start()

    def column(k, side):
        return lax.rem(outer + k, outer_count) * 2 + side

    def seq_peer(k):
        return lax.rem(row + k, seq_count)

    chan_peers = [partner] + [column(k, inner) for k in range(1, outer_count)]
    greet(chan_peers, [seq_peer(k) for k in range(1, seq_count)])

    buffers = (tok_all, cot_all)
    lines = ((0, inner), (1, inner), (1, 1 - inner))
    ways = (1, -1)

    def inside(place):
        return jnp.logical_and(place >= 0, place < outer_count)

    def owner_of(way, d, side):
        return (outer - way * d) * 2 + side

    def along(line, way, d):
        which, side = lines[line]
        owner = owner_of(way, d - 1, side)
        source = (tok, cot)[which] if d == 1 and line < 2 else buffers[which].at[owner]
        return pltpu.make_async_remote_copy(
            src_ref=source,
            dst_ref=buffers[which].at[owner],
            send_sem=line_send.at[line, 1 - max(way, 0), d],
            recv_sem=line_recv.at[line, 1 - max(way, 0), d],
            device_id={"chan": (outer + way) * 2 + inner},
            device_id_type=MESH,
        )

    def landed(line, way, d):
        which, side = lines[line]
        return pltpu.make_async_remote_copy(
            src_ref=buffers[which].at[owner_of(way, d, side)],
            dst_ref=buffers[which].at[owner_of(way, d, side)],
            send_sem=line_send.at[line, 1 - max(way, 0), d],
            recv_sem=line_recv.at[line, 1 - max(way, 0), d],
            device_id={"chan": (outer - way) * 2 + inner},
            device_id_type=MESH,
        )

    def sends(way, d):
        return jnp.logical_and(inside(outer - way * (d - 1)), inside(outer + way))

    def launch(line, d):
        for way in ways:
            @pl.when(sends(way, d))
            def _():
                along(line, way, d).start()

    def across(which, owner, slot):
        own = slot == 0
        return pltpu.make_async_remote_copy(
            src_ref=(tok, cot)[which] if own else buffers[which].at[owner],
            dst_ref=buffers[which].at[owner],
            send_sem=pair_send.at[which, slot],
            recv_sem=pair_recv.at[which, slot],
            device_id={"chan": partner},
            device_id_type=MESH,
        )

    def slot_of(way, d):
        return (1 - max(way, 0)) * (outer_count - 1) + d

    firsts = [across(which, me, 0) for which in range(2)]
    launch(0, 1)
    for copy in firsts:
        copy.start()

    def spread(source, target, where):
        copies = []
        for k in range(1, seq_count):
            peer = seq_peer(k)
            lanes = pl.ds(pl.multiple_of(peer * part, part), part)
            copies.append(
                pltpu.make_async_remote_copy(
                    src_ref=source.at[:, :, lanes],
                    dst_ref=target,
                    send_sem=seq_send.at[where, k],
                    recv_sem=seq_recv.at[where, k],
                    device_id={"seq": peer},
                    device_id_type=MESH,
                )
            )
        lanes = pl.ds(pl.multiple_of(row * part, part), part)
        own = pltpu.make_async_copy(source.at[:, :, lanes], target, own_sem.at[where])
        for copy in copies + [own]:
            copy.start()
        return copies + [own]

    def add_tok(block, owner, first=False):
        span = pl.ds(pl.multiple_of(owner * depth, depth), depth)
        for j in range(3):
            product = jnp.dot(block, w_all[j, span, :], preferred_element_type=jnp.float32)
            acc[j] = product if first else acc[j] + product

    def add_cot(block, owner, first=False):
        span = pl.ds(pl.multiple_of(owner * depth, depth), depth)
        product = lax.dot_general(
            block, ow_all[:, span], (((1,), (1,)), ((), ())), preferred_element_type=jnp.float32
        )
        grad[0] = product if first else grad[0] + product

    last = spread(filters, filt.at[:, row], 2)
    for load in loads[:3]:
        load.wait()
    add_tok(tok[...], me, True)

    def step(line, d):
        which, side = lines[line]
        for way in ways:
            @pl.when(inside(outer - way * d))
            def _():
                landed(line, way, d).wait_recv()
                if d + 1 < outer_count:
                    @pl.when(inside(outer + way))
                    def _():
                        along(line, way, d + 1).start()
                owner = owner_of(way, d, side)
                if line == 0:
                    across(0, owner, slot_of(way, d)).start()
                    add_tok(tok_all[owner], owner)
                else:
                    add_cot(cot_all[owner], owner)

    loads[3].wait()
    launch(1, 1)
    step(0, 1)
    firsts[1].wait_recv()
    launch(2, 1)
    add_cot(cot[...], me, True)
    add_cot(cot_all[partner], partner)
    firsts[0].wait_recv()
    add_tok(tok_all[partner], partner)
    for d in range(1, outer_count):
        if d > 1:
            step(0, d)
        step(1, d)
        step(2, d)
    for d in range(1, outer_count):
        for way in ways:
            @pl.when(inside(outer - way * d))
            def _():
                owner = owner_of(way, d, 1 - inner)
                across(0, owner, slot_of(way, d)).wait_recv()
                add_tok(tok_all[owner], owner)

    last = last + spread(acc, out.at[pl.ds(0, 3), row], 0)
    last = last + spread(grad, out.at[pl.ds(3, 1), row], 1)
    for copy in firsts:
        copy.wait_send()
    for d in range(1, outer_count):
        for way in ways:
            @pl.when(sends(way, d))
            def _():
                for line in range(3):
                    along(line, way, d).wait_send()

            @pl.when(inside(outer - way * d))
            def _():
                across(0, owner_of(way, d, inner), slot_of(way, d)).wait_send()

    for copy in last:
        copy.wait()


def project(tokens, cotangent, weights, out_weight, filters):
    chan_count, seq_count = lax.axis_size("chan"), lax.axis_size("seq")
    rows, depth = tokens.shape
    chans = weights.shape[2]
    vmem = pl.BlockSpec(memory_space=pltpu.VMEM)
    anywhere = pl.BlockSpec(memory_space=pl.ANY)
    return pl.pallas_call(
        functools.partial(project_kernel, chan_count, seq_count),
        out_shape=[
            jax.ShapeDtypeStruct((count, seq_count, rows, chans // seq_count), jnp.float32)
            for count in (4, 2)
        ],
        in_specs=[vmem, vmem, anywhere, anywhere, anywhere],
        out_specs=[vmem, vmem],
        scratch_shapes=[
            pltpu.VMEM((chan_count, rows, depth), jnp.bfloat16),
            pltpu.VMEM((chan_count, rows, depth), jnp.bfloat16),
            pltpu.VMEM(weights.shape, jnp.bfloat16),
            pltpu.VMEM(out_weight.shape, jnp.bfloat16),
            pltpu.VMEM((3, rows, chans), jnp.float32),
            pltpu.VMEM((1, rows, chans), jnp.float32),
            pltpu.SemaphoreType.DMA((4,)),
            pltpu.SemaphoreType.DMA((3, 2, chan_count // 2)),
            pltpu.SemaphoreType.DMA((3, 2, chan_count // 2)),
            pltpu.SemaphoreType.DMA((2, chan_count)),
            pltpu.SemaphoreType.DMA((2, chan_count)),
            pltpu.SemaphoreType.DMA((3, seq_count)),
            pltpu.SemaphoreType.DMA((3, seq_count)),
            pltpu.SemaphoreType.DMA((3,)),
        ],
        cost_estimate=pl.CostEstimate(
            flops=2 * rows * depth * chan_count * chans * 4,
            bytes_accessed=2 * depth * chan_count * chans * 4,
            transcendentals=0,
        ),
        compiler_params=pltpu.CompilerParams(
            collective_id=0, has_side_effects=True, vmem_limit_bytes=40 * 2**20
        ),
    )(tokens, cotangent, weights, out_weight, filters)


def split(value):
    high = value.astype(jnp.bfloat16)
    return high, (value - high.astype(jnp.float32)).astype(jnp.bfloat16)


def table_dot(high, low, value):
    top, rest = split(value)
    wide = jnp.dot(high, jnp.concatenate([top, rest], axis=1), preferred_element_type=jnp.float32)
    lanes = value.shape[1]
    small = jnp.dot(low, top, preferred_element_type=jnp.float32)
    return wide[:, :lanes] + (wide[:, lanes:] + small)


def middle_kernel(
    both, filters, taps, skip, high, low, back_high, back_low, second, grads, spec_one, spec_two
):
    length = filters.shape[1]
    count = taps.shape[0]
    rows = lax.broadcasted_iota(jnp.int32, filters.shape[1:], 0)

    def ahead(signal):
        return table_dot(high[...], low[...], signal)

    def conv(signal, spec, conjugate):
        product = times(ahead(signal), spec[...], conjugate)
        return table_dot(back_high[...], back_low[...], product) * (1.0 / length)

    def shifted(value, by):
        if by > 0:
            return jnp.where(rows < by, 0.0, pltpu.roll(value, by, 0))
        return jnp.where(rows >= length + by, 0.0, pltpu.roll(value, length + by, 0))

    def short(value, j, sign):
        total = taps[0, j : j + 1] * value
        for a in range(1, count):
            total = total + taps[a, j : j + 1] * shifted(value, sign * a)
        return total

    spec_one[...] = ahead(filters[0])
    spec_two[...] = ahead(filters[1])
    values, gate_one, gate_two = [short(both[j], j, 1) for j in range(3)]
    conv_one = conv(values, spec_one, False) + skip[0:1] * values
    first_out = gate_one * conv_one
    conv_two = conv(first_out, spec_two, False) + skip[1:2] * first_out
    second[...] = (gate_two * conv_two).astype(jnp.bfloat16)
    grads[2] = short(both[3] * conv_two, 2, -1).astype(jnp.bfloat16)
    grad_conv_two = both[3] * gate_two
    grad_first = conv(grad_conv_two, spec_two, True) + skip[1:2] * grad_conv_two
    grads[1] = short(grad_first * conv_one, 1, -1).astype(jnp.bfloat16)
    grad_conv_one = grad_first * gate_one
    grad_values = conv(grad_conv_one, spec_one, True) + skip[0:1] * grad_conv_one
    grads[0] = short(grad_values, 0, -1).astype(jnp.bfloat16)


def fused_middle(both, filters, taps, skip, table):
    length, lanes = filters.shape[1:]

    def halves(array):
        high = array.astype(jnp.bfloat16)
        return high, (array - high.astype(np.float32)).astype(jnp.bfloat16)

    tables = halves(table) + halves(np.ascontiguousarray(table.T))
    return pl.pallas_call(
        middle_kernel,
        out_shape=[
            jax.ShapeDtypeStruct((length, lanes), jnp.bfloat16),
            jax.ShapeDtypeStruct((3, length, lanes), jnp.bfloat16),
        ],
        in_specs=[pl.BlockSpec(memory_space=pltpu.VMEM)] * 8,
        out_specs=[pl.BlockSpec(memory_space=pltpu.VMEM)] * 2,
        scratch_shapes=[pltpu.VMEM((2 * length, lanes), jnp.float32)] * 2,
        compiler_params=pltpu.CompilerParams(vmem_limit_bytes=40 * 2**20),
    )(both, filters, taps, skip, *[jnp.asarray(t) for t in tables])


def output_kernel(
    chan_count, seq_count, sec, grads, w, ow, mixed, token_grad,
    sec_all, grads_all, w_all, ow_all, mine, sent, came, sum_sent, sum_came,
    w_sem, seq_send, seq_recv, pair_send, pair_recv, sum_send, sum_recv, own_sem,
):
    me, row = lax.axis_index("chan"), lax.axis_index("seq")
    outer_count = chan_count // 2
    outer, inner = me // 2, lax.rem(me, 2)
    partner = outer * 2 + 1 - inner
    depth = mixed.shape[1]
    part = sec.shape[2]
    loads = [pltpu.make_async_copy(ow, ow_all, w_sem.at[3])]
    loads = loads + [pltpu.make_async_copy(w.at[j], w_all.at[j], w_sem.at[j]) for j in range(3)]
    for load in loads:
        load.start()

    def column(k, side):
        return lax.rem(outer + k, outer_count) * 2 + side

    def seq_peer(k):
        return lax.rem(row + k, seq_count)

    chan_peers = [partner] + [column(k, inner) for k in range(1, outer_count)]
    greet(chan_peers, [seq_peer(k) for k in range(1, seq_count)])
    lanes = pl.ds(pl.multiple_of(row * part, part), part)
    targets = (sec_all.at[:, lanes], grads_all.at[:, :, lanes])

    def source(which, peer):
        return sec.at[peer] if which == 0 else grads.at[:, peer]

    moves = [[], []]
    for which in range(2):
        for k in range(1, seq_count):
            moves[which].append(
                pltpu.make_async_remote_copy(
                    src_ref=source(which, seq_peer(k)),
                    dst_ref=targets[which],
                    send_sem=seq_send.at[which, k],
                    recv_sem=seq_recv.at[which, k],
                    device_id={"seq": seq_peer(k)},
                    device_id_type=MESH,
                )
            )
        moves[which].append(
            pltpu.make_async_copy(source(which, row), targets[which], own_sem.at[which])
        )
        for move in moves[which]:
            move.start()

    def partial(which, owner):
        lines = pl.ds(pl.multiple_of(owner * depth, depth), depth)
        if which == 0:
            return jnp.dot(sec_all[...], ow_all[:, lines], preferred_element_type=jnp.float32)
        total = 0.0
        for j in range(3):
            total = total + lax.dot_general(
                grads_all[j],
                w_all[j, lines, :],
                (((1,), (1,)), ((), ())),
                preferred_element_type=jnp.float32,
            )
        return total

    pairs, sums = [{}, {}], [{}, {}]
    order = list(range(1, outer_count)) + [0]

    def make(which, k):
        sent[which, k] = partial(which, column(k, 1 - inner)).astype(jnp.bfloat16)
        pairs[which][k] = pltpu.make_async_remote_copy(
            src_ref=sent.at[which, k],
            dst_ref=came.at[which, k],
            send_sem=pair_send.at[which, k],
            recv_sem=pair_recv.at[which, k],
            device_id={"chan": partner},
            device_id_type=MESH,
        )
        pairs[which][k].start()
        mine[which, k] = partial(which, column(k, inner))

    def reduce_pair(which, k):
        pairs[which][k].wait_recv()
        total = mine[which, k] + came[which, k].astype(jnp.float32)
        if k == 0:
            mine[which, 0] = total
            return
        sum_sent[which, k] = total.astype(jnp.bfloat16)
        sums[which][k] = pltpu.make_async_remote_copy(
            src_ref=sum_sent.at[which, k],
            dst_ref=sum_came.at[which, k],
            send_sem=sum_send.at[which, k],
            recv_sem=sum_recv.at[which, k],
            device_id={"chan": column(k, inner)},
            device_id_type=MESH,
        )
        sums[which][k].start()

    def finish(which, out):
        total = mine[which, 0]
        for k in range(1, outer_count):
            sums[which][k].wait_recv()
            total = total + sum_came[which, k].astype(jnp.float32)
        out[...] = total.astype(jnp.bfloat16)

    for move in moves[0]:
        move.wait()
    loads[0].wait()
    for k in order:
        make(0, k)
    for move in moves[1]:
        move.wait()
    for load in loads[1:]:
        load.wait()
    for k in order:
        make(1, k)
        reduce_pair(0, k)
    for k in order:
        reduce_pair(1, k)
    finish(0, mixed)
    finish(1, token_grad)
    for which in range(2):
        for copy in list(pairs[which].values()) + list(sums[which].values()):
            copy.wait_send()


def output_sums(second, grads, weights, out_weight):
    chan_count, seq_count = lax.axis_size("chan"), lax.axis_size("seq")
    rows = second.shape[1]
    width, chans = weights.shape[1:]
    depth = width // chan_count
    outer_count = chan_count // 2
    vmem = pl.BlockSpec(memory_space=pltpu.VMEM)
    anywhere = pl.BlockSpec(memory_space=pl.ANY)
    block = (2, outer_count, rows, depth)
    return pl.pallas_call(
        functools.partial(output_kernel, chan_count, seq_count),
        out_shape=[jax.ShapeDtypeStruct((rows, depth), jnp.bfloat16)] * 2,
        in_specs=[vmem, vmem, anywhere, anywhere],
        out_specs=[vmem, vmem],
        scratch_shapes=[
            pltpu.VMEM((rows, chans), jnp.bfloat16),
            pltpu.VMEM((3, rows, chans), jnp.bfloat16),
            pltpu.VMEM(weights.shape, jnp.bfloat16),
            pltpu.VMEM(out_weight.shape, jnp.bfloat16),
            pltpu.VMEM(block, jnp.float32),
        ]
        + [pltpu.VMEM(block, jnp.bfloat16)] * 4
        + [
            pltpu.SemaphoreType.DMA((4,)),
            pltpu.SemaphoreType.DMA((2, seq_count)),
            pltpu.SemaphoreType.DMA((2, seq_count)),
        ]
        + [pltpu.SemaphoreType.DMA((2, outer_count))] * 4
        + [pltpu.SemaphoreType.DMA((2,))],
        compiler_params=pltpu.CompilerParams(
            collective_id=1, has_side_effects=True, vmem_limit_bytes=44 * 2**20
        ),
    )(second, grads, weights, out_weight)


def on_device(tokens, in_weight, short_kernel, filters, skip_gain, out_weight, cotangent):
    seq_count = lax.axis_size("seq")
    chans = in_weight.shape[2]
    part = chans // seq_count
    start = lax.axis_index("seq") * part
    weights = jnp.transpose(in_weight, (1, 0, 2))
    rows = tokens.shape[0]
    length = rows * seq_count
    table = odd_table(length)
    taps = lax.dynamic_slice_in_dim(short_kernel, start, part, 2)
    skip = lax.dynamic_slice_in_dim(skip_gain, start, part, 1)
    if part % 128 == 0 and rows % 16 == 0 and lax.axis_size("chan") % 2 == 0:
        both, local_filters = project(tokens, cotangent, weights, out_weight, filters)
        second_out, grads = fused_middle(
            both.reshape(4, length, part), local_filters.reshape(2, length, part), taps, skip, table
        )
        return output_sums(
            second_out.reshape(seq_count, rows, part),
            grads.reshape(3, seq_count, rows, part),
            weights,
            out_weight,
        )
    local_filters = swap_in(filters)
    gathered = lax.all_gather(tokens, "chan", axis=1, tiled=True)
    grad_rows = lax.all_gather(cotangent, "chan", axis=1, tiled=True)
    projected = jnp.stack(
        [jnp.dot(gathered, weights[j], preferred_element_type=jnp.float32) for j in range(3)]
    )
    grad_two = lax.dot_general(
        grad_rows, out_weight, (((1,), (1,)), ((), ())), preferred_element_type=jnp.float32
    )
    second_out, grads = middle(
        swap_in(projected), swap_in(grad_two), taps, local_filters, skip, jnp.asarray(table)
    )
    second_out = swap_out(second_out)
    grads = swap_out(grads)
    mixed = share(jnp.dot(second_out, out_weight, preferred_element_type=jnp.float32))
    total = 0.0
    for j in range(3):
        total = total + lax.dot_general(
            grads[j], weights[j], (((1,), (1,)), ((), ())), preferred_element_type=jnp.float32
        )
    return mixed, share(total)


def solution(mesh):
    in_specs = (
        P("seq", "chan"),
        P(None, None, "chan"),
        P(None, None, "chan"),
        P(None, "seq", "chan"),
        P(None, "chan"),
        P("chan", None),
        P("seq", "chan"),
    )
    out_specs = (P("seq", "chan"), P("seq", "chan"))
    return jax.shard_map(
        on_device, mesh=mesh, in_specs=in_specs, out_specs=out_specs, check_vma=False
    )
```

```python
import functools
import math

import jax
import jax.numpy as jnp
import numpy as np
from jax import lax
from jax.experimental import pallas as pl
from jax.experimental.pallas import tpu as pltpu
from jax.sharding import PartitionSpec as P

FINE = lax.Precision.HIGH


def odd_table(length):
    steps = np.arange(length, dtype=np.int64)
    turn = (2 * steps[:, None] + 1) * steps[None, :] % (4 * length)
    angle = turn.astype(np.float64) * (math.pi / (2 * length))
    return np.concatenate([np.cos(angle), -np.sin(angle)]).astype(np.float32)


def forward(table, signal):
    return jnp.dot(table, signal, precision=FINE)


def inverse(table, spec):
    length = table.shape[1]
    full = lax.dot_general(table, spec, (((0,), (0,)), ((), ())), precision=FINE)
    return full * (1.0 / length)


def times(left, right, conjugate):
    half = left.shape[0] // 2
    a, b = left[:half], left[half:]
    c, d = right[:half], right[half:]
    if conjugate:
        d = -d
    return jnp.concatenate([a * c - b * d, a * d + b * c])


def lag(array, by):
    return jnp.pad(array, ((by, 0), (0, 0)))[: array.shape[0]]


def lead(array, by):
    return jnp.pad(array, ((0, by), (0, 0)))[by:]


def middle(projected, grad_two, taps, filters, skip, table):
    count = taps.shape[0]
    shorted = []
    for j in range(3):
        total = taps[0, j] * projected[j]
        for a in range(1, count):
            total = total + taps[a, j] * lag(projected[j], a)
        shorted.append(total)
    values, gate_one, gate_two = shorted
    spec_one = forward(table, filters[0])
    spec_two = forward(table, filters[1])
    conv_one = inverse(table, times(forward(table, values), spec_one, False)) + skip[0] * values
    first_out = gate_one * conv_one
    conv_two = (
        inverse(table, times(forward(table, first_out), spec_two, False)) + skip[1] * first_out
    )
    second_out = (gate_two * conv_two).astype(jnp.bfloat16)
    grad_gate_two = grad_two * conv_two
    grad_conv_two = grad_two * gate_two
    grad_first = (
        inverse(table, times(forward(table, grad_conv_two), spec_two, True))
        + skip[1] * grad_conv_two
    )
    grad_gate_one = grad_first * conv_one
    grad_conv_one = grad_first * gate_one
    grad_values = (
        inverse(table, times(forward(table, grad_conv_one), spec_one, True))
        + skip[0] * grad_conv_one
    )
    grads = []
    for j, g in enumerate((grad_values, grad_gate_one, grad_gate_two)):
        total = taps[0, j] * g
        for a in range(1, count):
            total = total + taps[a, j] * lead(g, a)
        grads.append(total.astype(jnp.bfloat16))
    return second_out, jnp.stack(grads)


def swap_in(array):
    return lax.all_to_all(array, "seq", array.ndim - 1, array.ndim - 2, tiled=True)


def swap_out(array):
    return lax.all_to_all(array, "seq", array.ndim - 2, array.ndim - 1, tiled=True)


def share(partial):
    count = lax.axis_size("chan")
    rows, width = partial.shape
    sent = partial.astype(jnp.bfloat16).reshape(rows, count, width // count).transpose(1, 0, 2)
    got = lax.all_to_all(sent, "chan", 0, 0, tiled=True)
    return jnp.sum(got.astype(jnp.float32), axis=0).astype(jnp.bfloat16)


MESH = pl.DeviceIdType.MESH


def greet(chan_peers, seq_peers):
    barrier = pltpu.get_barrier_semaphore()
    for axis, peers in (("chan", chan_peers), ("seq", seq_peers)):
        for peer in peers:
            pl.semaphore_signal(barrier, inc=1, device_id={axis: peer}, device_id_type=MESH)
    pl.semaphore_wait(barrier, len(chan_peers) + len(seq_peers))


def project_kernel(
    chan_count, seq_count, tok, cot, w, ow, filters, out, filt,
    tok_all, cot_all, w_all, ow_all, acc, grad,
    w_sem, send_sem, recv_sem, seq_send, seq_recv, own_sem,
):
    me, row = lax.axis_index("chan"), lax.axis_index("seq")
    outer_count = chan_count // 2
    outer, inner = me // 2, lax.rem(me, 2)
    partner = outer * 2 + 1 - inner
    depth = tok.shape[1]
    part = out.shape[3]
    loads = [pltpu.make_async_copy(w.at[j], w_all.at[j], w_sem.at[j]) for j in range(3)]
    loads.append(pltpu.make_async_copy(ow, ow_all, w_sem.at[3]))
    loads.append(pltpu.make_async_copy(tok, tok_all.at[me], w_sem.at[4]))
    loads.append(pltpu.make_async_copy(cot, cot_all.at[me], w_sem.at[5]))
    for load in loads[4:] + loads[:4]:
        load.start()

    def column(k, side):
        return lax.rem(outer + k + outer_count, outer_count) * 2 + side

    def seq_peer(k):
        return lax.rem(row + k, seq_count)

    chan_peers = [partner] + [column(k, inner) for k in range(1, outer_count)]
    greet(chan_peers, [seq_peer(k) for k in range(1, seq_count)])

    def push(which, source, target, owner, slot):
        place = (tok_all, cot_all)[which].at[owner]
        return pltpu.make_async_remote_copy(
            src_ref=source,
            dst_ref=place,
            send_sem=send_sem.at[which, slot],
            recv_sem=recv_sem.at[which, slot],
            device_id={"chan": target},
            device_id_type=MESH,
        )

    held = [{}, {}]

    def spread(source, target, where):
        copies = []
        for k in range(1, seq_count):
            peer = seq_peer(k)
            lanes = pl.ds(pl.multiple_of(peer * part, part), part)
            copies.append(
                pltpu.make_async_remote_copy(
                    src_ref=source.at[:, :, lanes],
                    dst_ref=target,
                    send_sem=seq_send.at[where, k],
                    recv_sem=seq_recv.at[where, k],
                    device_id={"seq": peer},
                    device_id_type=MESH,
                )
            )
        lanes = pl.ds(pl.multiple_of(row * part, part), part)
        own = pltpu.make_async_copy(source.at[:, :, lanes], target, own_sem.at[where])
        for copy in copies + [own]:
            copy.start()
        return copies + [own]

    for which, source in enumerate((tok, cot)):
        for k in range(1, outer_count):
            held[which][k] = push(which, source, column(k, inner), me, k)
        held[which][0] = push(which, source, partner, me, 0)
        for copy in held[which].values():
            copy.start()

    def pass_on(which, k):
        held[which][k].wait_recv()
        owner = column(-k, inner)
        slot = outer_count - 1 + k
        held[which][slot] = push(which, (tok_all, cot_all)[which].at[owner], partner, owner, slot)
        held[which][slot].start()
        return owner

    def add_tok(block, owner, first=False):
        lines = pl.ds(pl.multiple_of(owner * depth, depth), depth)
        for j in range(3):
            product = jnp.dot(block, w_all[j, lines, :], preferred_element_type=jnp.float32)
            acc[j] = product if first else acc[j] + product

    def add_cot(block, owner, first=False):
        lines = pl.ds(pl.multiple_of(owner * depth, depth), depth)
        product = lax.dot_general(
            block, ow_all[:, lines], (((1,), (1,)), ((), ())), preferred_element_type=jnp.float32
        )
        grad[0] = product if first else grad[0] + product

    last = spread(filters, filt.at[:, row], 2)
    for load in loads[:3] + [loads[4]]:
        load.wait()
    add_tok(tok_all[me], me, True)
    for k in range(1, outer_count):
        owner = pass_on(0, k)
        add_tok(tok_all[owner], owner)
    held[0][0].wait_recv()
    add_tok(tok_all[partner], partner)
    loads[3].wait()
    loads[5].wait()
    add_cot(cot_all[me], me, True)
    for k in range(1, outer_count):
        owner = pass_on(1, k)
        add_cot(cot_all[owner], owner)
        held[0][outer_count - 1 + k].wait_recv()
        owner = column(-k, 1 - inner)
        add_tok(tok_all[owner], owner)

    last = last + spread(acc, out.at[pl.ds(0, 3), row], 0)
    held[1][0].wait_recv()
    add_cot(cot_all[partner], partner)
    for k in range(1, outer_count):
        held[1][outer_count - 1 + k].wait_recv()
        owner = column(-k, 1 - inner)
        add_cot(cot_all[owner], owner)
    last = last + spread(grad, out.at[pl.ds(3, 1), row], 1)
    for copies in held:
        for copy in copies.values():
            copy.wait_send()
    for copy in last:
        copy.wait()


def project(tokens, cotangent, weights, out_weight, filters):
    chan_count, seq_count = lax.axis_size("chan"), lax.axis_size("seq")
    rows, depth = tokens.shape
    chans = weights.shape[2]
    vmem = pl.BlockSpec(memory_space=pltpu.VMEM)
    anywhere = pl.BlockSpec(memory_space=pl.ANY)
    return pl.pallas_call(
        functools.partial(project_kernel, chan_count, seq_count),
        out_shape=[
            jax.ShapeDtypeStruct((count, seq_count, rows, chans // seq_count), jnp.float32)
            for count in (4, 2)
        ],
        in_specs=[anywhere] * 5,
        out_specs=[vmem, vmem],
        scratch_shapes=[
            pltpu.VMEM((chan_count, rows, depth), jnp.bfloat16),
            pltpu.VMEM((chan_count, rows, depth), jnp.bfloat16),
            pltpu.VMEM(weights.shape, jnp.bfloat16),
            pltpu.VMEM(out_weight.shape, jnp.bfloat16),
            pltpu.VMEM((3, rows, chans), jnp.float32),
            pltpu.VMEM((1, rows, chans), jnp.float32),
            pltpu.SemaphoreType.DMA((6,)),
            pltpu.SemaphoreType.DMA((2, chan_count)),
            pltpu.SemaphoreType.DMA((2, chan_count)),
            pltpu.SemaphoreType.DMA((3, seq_count)),
            pltpu.SemaphoreType.DMA((3, seq_count)),
            pltpu.SemaphoreType.DMA((3,)),
        ],
        cost_estimate=pl.CostEstimate(
            flops=2 * rows * depth * chan_count * chans * 4,
            bytes_accessed=2 * depth * chan_count * chans * 4,
            transcendentals=0,
        ),
        compiler_params=pltpu.CompilerParams(
            collective_id=0, has_side_effects=True, vmem_limit_bytes=55 * 2**20
        ),
    )(tokens, cotangent, weights, out_weight, filters)


def split(value):
    high = value.astype(jnp.bfloat16)
    return high, (value - high.astype(jnp.float32)).astype(jnp.bfloat16)


def table_dot(high, low, value):
    top, rest = split(value)
    wide = jnp.dot(high, jnp.concatenate([top, rest], axis=1), preferred_element_type=jnp.float32)
    lanes = value.shape[1]
    small = jnp.dot(low, top, preferred_element_type=jnp.float32)
    return wide[:, :lanes] + (wide[:, lanes:] + small)


def middle_kernel(
    both, filters, taps, skip, high, low, back_high, back_low, second, grads, spec_one, spec_two
):
    length = filters.shape[1]
    count = taps.shape[0]
    rows = lax.broadcasted_iota(jnp.int32, filters.shape[1:], 0)

    def ahead(signal):
        return table_dot(high[...], low[...], signal)

    def conv(signal, spec, conjugate):
        product = times(ahead(signal), spec[...], conjugate)
        return table_dot(back_high[...], back_low[...], product) * (1.0 / length)

    def shifted(value, by):
        if by > 0:
            return jnp.where(rows < by, 0.0, pltpu.roll(value, by, 0))
        return jnp.where(rows >= length + by, 0.0, pltpu.roll(value, length + by, 0))

    def short(value, j, sign):
        total = taps[0, j : j + 1] * value
        for a in range(1, count):
            total = total + taps[a, j : j + 1] * shifted(value, sign * a)
        return total

    spec_one[...] = ahead(filters[0])
    spec_two[...] = ahead(filters[1])
    values, gate_one, gate_two = [short(both[j], j, 1) for j in range(3)]
    conv_one = conv(values, spec_one, False) + skip[0:1] * values
    first_out = gate_one * conv_one
    conv_two = conv(first_out, spec_two, False) + skip[1:2] * first_out
    second[...] = (gate_two * conv_two).astype(jnp.bfloat16)
    grads[2] = short(both[3] * conv_two, 2, -1).astype(jnp.bfloat16)
    grad_conv_two = both[3] * gate_two
    grad_first = conv(grad_conv_two, spec_two, True) + skip[1:2] * grad_conv_two
    grads[1] = short(grad_first * conv_one, 1, -1).astype(jnp.bfloat16)
    grad_conv_one = grad_first * gate_one
    grad_values = conv(grad_conv_one, spec_one, True) + skip[0:1] * grad_conv_one
    grads[0] = short(grad_values, 0, -1).astype(jnp.bfloat16)


def fused_middle(both, filters, taps, skip, table):
    length, lanes = filters.shape[1:]

    def halves(array):
        high = array.astype(jnp.bfloat16)
        return high, (array - high.astype(np.float32)).astype(jnp.bfloat16)

    tables = halves(table) + halves(np.ascontiguousarray(table.T))
    return pl.pallas_call(
        middle_kernel,
        out_shape=[
            jax.ShapeDtypeStruct((length, lanes), jnp.bfloat16),
            jax.ShapeDtypeStruct((3, length, lanes), jnp.bfloat16),
        ],
        in_specs=[pl.BlockSpec(memory_space=pltpu.VMEM)] * 8,
        out_specs=[pl.BlockSpec(memory_space=pltpu.VMEM)] * 2,
        scratch_shapes=[pltpu.VMEM((2 * length, lanes), jnp.float32)] * 2,
        compiler_params=pltpu.CompilerParams(vmem_limit_bytes=40 * 2**20),
    )(both, filters, taps, skip, *[jnp.asarray(t) for t in tables])


def output_kernel(
    chan_count, seq_count, sec, grads, w, ow, mixed, token_grad,
    sec_all, grads_all, w_all, ow_all, mine, sent, came, sum_sent, sum_came,
    w_sem, seq_send, seq_recv, pair_send, pair_recv, sum_send, sum_recv, own_sem,
):
    me, row = lax.axis_index("chan"), lax.axis_index("seq")
    outer_count = chan_count // 2
    outer, inner = me // 2, lax.rem(me, 2)
    partner = outer * 2 + 1 - inner
    depth = mixed.shape[1]
    part = sec.shape[2]
    loads = [pltpu.make_async_copy(ow, ow_all, w_sem.at[3])]
    loads = loads + [pltpu.make_async_copy(w.at[j], w_all.at[j], w_sem.at[j]) for j in range(3)]
    for load in loads:
        load.start()

    def column(k, side):
        return lax.rem(outer + k, outer_count) * 2 + side

    def seq_peer(k):
        return lax.rem(row + k, seq_count)

    chan_peers = [partner] + [column(k, inner) for k in range(1, outer_count)]
    greet(chan_peers, [seq_peer(k) for k in range(1, seq_count)])
    lanes = pl.ds(pl.multiple_of(row * part, part), part)
    targets = (sec_all.at[:, lanes], grads_all.at[:, :, lanes])

    def source(which, peer):
        return sec.at[peer] if which == 0 else grads.at[:, peer]

    moves = [[], []]
    for which in range(2):
        for k in range(1, seq_count):
            moves[which].append(
                pltpu.make_async_remote_copy(
                    src_ref=source(which, seq_peer(k)),
                    dst_ref=targets[which],
                    send_sem=seq_send.at[which, k],
                    recv_sem=seq_recv.at[which, k],
                    device_id={"seq": seq_peer(k)},
                    device_id_type=MESH,
                )
            )
        moves[which].append(
            pltpu.make_async_copy(source(which, row), targets[which], own_sem.at[which])
        )
        for move in moves[which]:
            move.start()

    def partial(which, owner):
        lines = pl.ds(pl.multiple_of(owner * depth, depth), depth)
        if which == 0:
            return jnp.dot(sec_all[...], ow_all[:, lines], preferred_element_type=jnp.float32)
        total = 0.0
        for j in range(3):
            total = total + lax.dot_general(
                grads_all[j],
                w_all[j, lines, :],
                (((1,), (1,)), ((), ())),
                preferred_element_type=jnp.float32,
            )
        return total

    pairs, sums = [{}, {}], [{}, {}]
    order = list(range(1, outer_count)) + [0]

    def make(which, k):
        sent[which, k] = partial(which, column(k, 1 - inner)).astype(jnp.bfloat16)
        pairs[which][k] = pltpu.make_async_remote_copy(
            src_ref=sent.at[which, k],
            dst_ref=came.at[which, k],
            send_sem=pair_send.at[which, k],
            recv_sem=pair_recv.at[which, k],
            device_id={"chan": partner},
            device_id_type=MESH,
        )
        pairs[which][k].start()
        mine[which, k] = partial(which, column(k, inner))

    def reduce_pair(which, k):
        pairs[which][k].wait_recv()
        total = mine[which, k] + came[which, k].astype(jnp.float32)
        if k == 0:
            mine[which, 0] = total
            return
        sum_sent[which, k] = total.astype(jnp.bfloat16)
        sums[which][k] = pltpu.make_async_remote_copy(
            src_ref=sum_sent.at[which, k],
            dst_ref=sum_came.at[which, k],
            send_sem=sum_send.at[which, k],
            recv_sem=sum_recv.at[which, k],
            device_id={"chan": column(k, inner)},
            device_id_type=MESH,
        )
        sums[which][k].start()

    def finish(which, out):
        total = mine[which, 0]
        for k in range(1, outer_count):
            sums[which][k].wait_recv()
            total = total + sum_came[which, k].astype(jnp.float32)
        out[...] = total.astype(jnp.bfloat16)

    for move in moves[0]:
        move.wait()
    loads[0].wait()
    for k in order:
        make(0, k)
    for move in moves[1]:
        move.wait()
    for load in loads[1:]:
        load.wait()
    for k in order:
        make(1, k)
        reduce_pair(0, k)
    for k in order:
        reduce_pair(1, k)
    finish(0, mixed)
    finish(1, token_grad)
    for which in range(2):
        for copy in list(pairs[which].values()) + list(sums[which].values()):
            copy.wait_send()


def output_sums(second, grads, weights, out_weight):
    chan_count, seq_count = lax.axis_size("chan"), lax.axis_size("seq")
    rows = second.shape[1]
    width, chans = weights.shape[1:]
    depth = width // chan_count
    outer_count = chan_count // 2
    vmem = pl.BlockSpec(memory_space=pltpu.VMEM)
    anywhere = pl.BlockSpec(memory_space=pl.ANY)
    block = (2, outer_count, rows, depth)
    return pl.pallas_call(
        functools.partial(output_kernel, chan_count, seq_count),
        out_shape=[jax.ShapeDtypeStruct((rows, depth), jnp.bfloat16)] * 2,
        in_specs=[vmem, vmem, anywhere, anywhere],
        out_specs=[vmem, vmem],
        scratch_shapes=[
            pltpu.VMEM((rows, chans), jnp.bfloat16),
            pltpu.VMEM((3, rows, chans), jnp.bfloat16),
            pltpu.VMEM(weights.shape, jnp.bfloat16),
            pltpu.VMEM(out_weight.shape, jnp.bfloat16),
            pltpu.VMEM(block, jnp.float32),
        ]
        + [pltpu.VMEM(block, jnp.bfloat16)] * 4
        + [
            pltpu.SemaphoreType.DMA((4,)),
            pltpu.SemaphoreType.DMA((2, seq_count)),
            pltpu.SemaphoreType.DMA((2, seq_count)),
        ]
        + [pltpu.SemaphoreType.DMA((2, outer_count))] * 4
        + [pltpu.SemaphoreType.DMA((2,))],
        compiler_params=pltpu.CompilerParams(
            collective_id=1, has_side_effects=True, vmem_limit_bytes=58 * 2**20
        ),
    )(second, grads, weights, out_weight)


def on_device(tokens, in_weight, short_kernel, filters, skip_gain, out_weight, cotangent):
    seq_count = lax.axis_size("seq")
    chans = in_weight.shape[2]
    part = chans // seq_count
    start = lax.axis_index("seq") * part
    weights = jnp.transpose(in_weight, (1, 0, 2))
    rows = tokens.shape[0]
    length = rows * seq_count
    table = odd_table(length)
    taps = lax.dynamic_slice_in_dim(short_kernel, start, part, 2)
    skip = lax.dynamic_slice_in_dim(skip_gain, start, part, 1)
    if part % 128 == 0 and rows % 16 == 0 and lax.axis_size("chan") % 2 == 0:
        both, local_filters = project(tokens, cotangent, weights, out_weight, filters)
        second_out, grads = fused_middle(
            both.reshape(4, length, part), local_filters.reshape(2, length, part), taps, skip, table
        )
        return output_sums(
            second_out.reshape(seq_count, rows, part),
            grads.reshape(3, seq_count, rows, part),
            weights,
            out_weight,
        )
    local_filters = swap_in(filters)
    gathered = lax.all_gather(tokens, "chan", axis=1, tiled=True)
    grad_rows = lax.all_gather(cotangent, "chan", axis=1, tiled=True)
    projected = jnp.stack(
        [jnp.dot(gathered, weights[j], preferred_element_type=jnp.float32) for j in range(3)]
    )
    grad_two = lax.dot_general(
        grad_rows, out_weight, (((1,), (1,)), ((), ())), preferred_element_type=jnp.float32
    )
    second_out, grads = middle(
        swap_in(projected), swap_in(grad_two), taps, local_filters, skip, jnp.asarray(table)
    )
    second_out = swap_out(second_out)
    grads = swap_out(grads)
    mixed = share(jnp.dot(second_out, out_weight, preferred_element_type=jnp.float32))
    total = 0.0
    for j in range(3):
        total = total + lax.dot_general(
            grads[j], weights[j], (((1,), (1,)), ((), ())), preferred_element_type=jnp.float32
        )
    return mixed, share(total)


def solution(mesh):
    in_specs = (
        P("seq", "chan"),
        P(None, None, "chan"),
        P(None, None, "chan"),
        P(None, "seq", "chan"),
        P(None, "chan"),
        P("chan", None),
        P("seq", "chan"),
    )
    out_specs = (P("seq", "chan"), P("seq", "chan"))
    return jax.shard_map(
        on_device, mesh=mesh, in_specs=in_specs, out_specs=out_specs, check_vma=False
    )
```
